256 devices in a mesh: seq: 32 (over y_hi, z, core), head: 8 (over y_lo, x).
Axes of the slice: x: 4, y: 4 (y_hi: 2, y_lo: 2; y = y_hi * 2 + y_lo), z: 8, core: 2. Of those that a mesh axis runs over, the one named last changes fastest.
Arguments:
- queries: bfloat16 [8192, 8192], P('seq', 'head'), parts along dimension 1, may hold values from -180 to 180
- keys: bfloat16 [8192, 1024], P('seq', 'head'), parts along dimension 1, may hold values from -6 to 6
- values: bfloat16 [8192, 1024], P('seq', 'head'), parts along dimension 1, may hold values from -6 to 6
- lengths: int32 [16], replicated, may hold values from 1 to 4608, 8192 in all
Outputs:
- attended: bfloat16 [8192, 8192], P('seq', 'head'), parts along dimension 1
The draws below stay inside these ranges and needn't reach their ends.
There are 8 independent parts, one for each index of `head`. The reference program is written for one: setup_inputs(seed, part) draws one part's arguments, and reference() takes and returns one part's arrays. A program takes and returns all parts, laid end to end along the dimension named above; an argument that names none is the same for every part. Nothing has to cross between parts.
Inputs may be any that keep to these rules, and one draw needn't show every extreme that they name: Document lengths sum to 8192; the longest is exactly 4608.
All inputs are finite; a program needn't handle non-finite values.
Results may differ from the reference program's by a relative error of at most 0.0045.
Values may be sent and summed in bfloat16 or wider, within the bound.
A program may use at most 64 MiB of HBM per device.

```python
import math
import jax
import jax.numpy as jnp
import numpy as np
from jax import lax

HQ = 8
DH = 128
NDOC = 16
TOKENS = 8192
MOST = 4608


def shared_base(key):
    return jnp.clip(jax.random.normal(key, (TOKENS, DH), jnp.float32), -6.0, 6.0)


def draw_keys(key, part):
    base = shared_base(key)
    return base.astype(jnp.bfloat16)


def draw_queries(key, part):
    key = jax.random.fold_in(key, 5)
    first = jax.random.fold_in(key, 0)
    fresh = jnp.clip(jax.random.normal(first, (TOKENS, HQ, DH), jnp.float32), -6.0, 6.0)
    return fresh.reshape(TOKENS, HQ * DH).astype(jnp.bfloat16)


def level_of(key, shape, pieces, smallest, top_value):
    loudness, own = 1.0, jax.random.fold_in(key, 6)
    for position, blocks in pieces:
        draws = jnp.exp(jax.random.uniform(jax.random.fold_in(own, position), (blocks,), jnp.float32, smallest / len(pieces), top_value / len(pieces)))
        loudness = loudness * jnp.repeat(draws, shape[position] // blocks).reshape([-1 if axis == position else 1 for axis in range(len(shape))])
    return loudness


def profile(count, total, bound, slope):
    portions = [(1 << 20) // math.isqrt(grade ** slope) + 1 for grade in range(2, count + 1)]
    surplus, counts = total - bound - (count - 1), [1] * (count - 1)
    while surplus > 0:
        free = [i for i in range(count - 1) if counts[i] < bound]
        mass, left = sum([portions[i] for i in free]), surplus
        for i in free:
            more = min(bound - counts[i], max(1, left * portions[i] // mass), surplus)
            counts[i] = counts[i] + more
            surplus = surplus - more
    return np.array([bound] + counts)


def ragged_sizes(own_key, amount, total, bound, lean):
    if amount == 2:
        one = jax.random.randint(own_key, (), max(1, total - bound), min(bound, total - 1) + 1)
        return jnp.stack([one, total - one])
    tallies = jnp.asarray(profile(amount, total, bound, lean), jnp.int32)
    couples = (amount - 1) // 2
    source_of, receiver = tallies[1:1 + 2 * couples:2], tallies[2:2 + 2 * couples:2]
    slack = jnp.minimum(source_of - 1, bound - receiver)
    shifted = jax.random.randint(jax.random.fold_in(own_key, 1), (couples,), 0, 1 << 20) % (slack + 1)
    tallies = tallies.at[1:1 + 2 * couples:2].set(source_of - shifted).at[2:2 + 2 * couples:2].set(receiver + shifted)
    return tallies[jax.random.permutation(jax.random.fold_in(own_key, 2), amount)]


def bell_draw(own_key, shape, spread, most, pieces=(), held_as=jnp.bfloat16):
    gain = level_of(own_key, shape, pieces, -0.22, 0.18) if pieces else 1.0
    result = jax.random.normal(own_key, shape, jnp.float32) * spread * gain
    return jnp.minimum(jnp.maximum(result, -most), most).astype(held_as)


def setup_inputs(seed: int = 0, part: int = 0) -> dict:
    arg_keys = jax.random.split(jax.random.key(seed), 5)
    part_keys = jax.random.split(jax.random.fold_in(arg_keys[4], part), 5)
    queries = draw_queries(jax.random.fold_in(jax.random.fold_in(arg_keys[4], part), 71), part)
    keys = draw_keys(jax.random.fold_in(jax.random.fold_in(arg_keys[4], part), 71), part)
    values = bell_draw(part_keys[2], (TOKENS, DH), 1.0, 6.0, ((0, 32),))
    lengths = ragged_sizes(arg_keys[3], NDOC, TOKENS, MOST, 2).astype(jnp.int32)
    return dict(queries=queries, keys=keys, values=values, lengths=lengths)


def doc_index(positions, lengths):
    ends = jnp.cumsum(lengths).astype(jnp.int32)
    return lax.optimization_barrier(jnp.sum((positions[:, None] >= ends[None, :]).astype(jnp.int32), axis=1)).astype(jnp.int32)

def reference(queries, keys, values, lengths):
    block = math.gcd(TOKENS, 512)
    scale = 1.0 / math.sqrt(DH)
    positions = jnp.arange(TOKENS, dtype=jnp.int32)
    docs = doc_index(positions, lengths)
    keys_f = keys.astype(jnp.float32)
    values_f = values.astype(jnp.float32)

    def one_block(number):
        begin = (number * block).astype(jnp.int32)
        query_block = lax.dynamic_slice_in_dim(queries, begin, block, 0).reshape(block, HQ, DH).astype(jnp.float32)
        query_pos = begin + jnp.arange(block, dtype=jnp.int32)
        query_doc = lax.dynamic_slice_in_dim(docs, begin, block, 0)
        scores = jnp.einsum('thd,kd->thk', query_block, keys_f) * scale
        allowed = (positions[None, :] <= query_pos[:, None]) & (docs[None, :] == query_doc[:, None])
        masked = jnp.where(allowed[:, None, :], scores, jnp.float32(-1e+30))
        top = lax.optimization_barrier(jnp.max(masked, axis=2, keepdims=True))
        weights = jnp.where(allowed[:, None, :], jnp.exp(scores - top), jnp.float32(0.0))
        total = lax.optimization_barrier(jnp.sum(weights, axis=2))
        rounded = lax.optimization_barrier(weights.astype(jnp.bfloat16)).astype(jnp.float32)
        mixed = jnp.einsum('thk,kd->thd', rounded, values_f)
        return (mixed / total[:, :, None]).reshape(block, HQ * DH).astype(jnp.bfloat16)
    blocks = lax.map(one_block, jnp.arange(TOKENS // block, dtype=jnp.int32))
    return blocks.reshape(TOKENS, HQ * DH)
```

```python
import functools
import math

import jax
import jax.numpy as jnp
from jax import lax
from jax.experimental import pallas as pl
from jax.experimental.pallas import tpu as pltpu
from jax.sharding import PartitionSpec as P

MESH = pl.DeviceIdType.MESH
HQ = 8
DH = 128
NDOC = 16
ROWS = 256
CHIPS = 16
CHUNKS = 4
PART = ROWS // CHUNKS
ROUNDS = 4
NONE = 31
FAR = -(2.0**20)
SCALE = math.log2(math.e) / math.sqrt(DH)

IN_WORDS = (
    (31969, 65504, 64833, 65506, 65507, 65508, 65509, 97472, 64800, 100392, 97385, 97418, 97451, 97484, 97517, 97736),
    (32767, 32746, 65504, 65505, 65506, 65507, 97284, 97441, 97506, 97376, 99464, 101545, 101578, 102635, 103692, 104873),
    (31818, 32767, 32767, 65504, 65505, 97282, 97315, 65508, 99523, 97415, 97442, 100552, 102633, 103690, 104747, 71047),
    (32767, 32767, 32767, 32767, 65504, 65505, 65506, 97378, 97444, 97446, 97479, 65511, 65512, 65513, 65514, 97611),
)
OUT_WORDS = (
    (1015808, 1016865, 98274, 131043, 163812, 196581, 229350, 262119, 1047816, 1047849, 1027050, 1048555, 1048556, 1048557, 1048558, 1048575),
    (1023039, 1048544, 1017153, 1019874, 1019875, 1020900, 1021925, 1021983, 1047840, 1047624, 1047657, 1047690, 1047723, 1047756, 1047789, 1047839),
    (1017855, 1047903, 1048544, 1018849, 1020898, 1021923, 1021956, 1020991, 1018087, 1047650, 1047688, 1047721, 1047754, 1047787, 1047820, 1047846),
    (359519, 1048575, 1048575, 1048544, 1048545, 1048546, 1048547, 1048575, 1048550, 1047687, 1047743, 1047752, 1047785, 1048554, 1048555, 1048549),
)

NT = (((1,), (1,)), ((), ()))


def pick(table, index, default=None):
    value = jnp.int32(table[0]) if default is None else jnp.int32(default)
    for number in range(0 if default is not None else 1, len(table)):
        value = jnp.where(index == number, table[number], value)
    return value


def field(word, place):
    return (word // 32**place) % 32


def kernel(
    queries_hbm, keys_hbm, values_hbm, lengths_ref, out_ref,
    q_ref, kv, far, mine, top, acc,
    q_sem, own_sem, recv_sem, sib_recv, send_sem, sib_send,
):
    seq, head = lax.axis_index("seq"), lax.axis_index("head")
    core = seq % 2
    chip = seq // 2
    z = chip % 8
    high = chip // 8
    own = 2 * chip + core

    def device(high, z, core):
        return (high * 16 + ((z + 8) % 8) * 2 + core, head)

    sibling = device(high, z, 1 - core)
    across = device(1 - high, z, core)
    slant = device(1 - high, z - 1 + 2 * high, core)
    edges = (device(high, z + 1, core), device(high, z - 1, core), across, slant)

    barrier = pltpu.get_barrier_semaphore()
    for other in edges + (sibling,):
        pl.semaphore_signal(barrier, inc=1, device_id=other, device_id_type=MESH)

    load_q = pltpu.make_async_copy(queries_hbm, q_ref, q_sem)
    load_q.start()
    for chunk in range(CHUNKS):
        part = pl.ds(chunk * PART, PART)
        pltpu.make_async_copy(keys_hbm.at[part], kv.at[own, chunk, 0], own_sem).start()
        pltpu.make_async_copy(values_hbm.at[part], kv.at[own, chunk, 1], own_sem).start()

    ins = [pick(row, chip) for row in IN_WORDS]
    outs = [pick(row, chip) for row in OUT_WORDS]

    lane = lax.broadcasted_iota(jnp.int32, (1, DH), 1)
    first = jnp.zeros((1, DH), jnp.int32)
    last = jnp.zeros((1, DH), jnp.int32)
    begin = jnp.int32(0)
    for number in range(NDOC):
        end = begin + lengths_ref[number]
        first = jnp.where(lane == number, begin, first)
        last = jnp.where(lane == number, end, last)
        begin = end

    row_pos = own * ROWS + lax.broadcasted_iota(jnp.int32, (ROWS, DH), 0)
    mine[...] = ((row_pos >= first) & (row_pos < last)).astype(jnp.float32).astype(jnp.bfloat16)

    @pl.loop(0, CHIPS)
    def _(block):
        pos = block * 2 * ROWS + lax.broadcasted_iota(jnp.int32, (2 * ROWS, DH), 0)
        inside = (pos >= first) & (pos < last)
        far[block] = jnp.where(inside | (lane >= NDOC), 0.0, FAR).astype(jnp.bfloat16)

    pltpu.make_async_copy(kv.at[own], kv.at[own], own_sem).wait()
    pl.semaphore_wait(barrier, 5)

    def sib_copy(block, chunk, sem):
        part = kv.at[2 * block + core, chunk]
        return pltpu.make_async_remote_copy(
            src_ref=part, dst_ref=part, send_sem=sem, recv_sem=sib_recv.at[block],
            device_id=sibling, device_id_type=MESH,
        )

    def sib_whole(block, sem):
        part = kv.at[2 * block + 1 - core]
        return pltpu.make_async_remote_copy(
            src_ref=part, dst_ref=part, send_sem=sem, recv_sem=sib_recv.at[block],
            device_id=sibling, device_id_type=MESH,
        )

    def edge_copy(edge, block, chunk, sem):
        part = kv.at[2 * block + core, chunk]
        return pltpu.make_async_remote_copy(
            src_ref=part, dst_ref=part, send_sem=sem, recv_sem=recv_sem.at[block, chunk],
            device_id=edges[edge], device_id_type=MESH,
        )

    def receive(number, word, chunk):
        needed = word // 32768
        for place in range(3):
            block = field(word, place)

            @pl.when(block < CHIPS)
            def _():
                edge_copy(0, block, chunk, send_sem.at[0, 0]).wait_recv()

            @pl.when(place < needed)
            def _():
                sib_copy(block, chunk, sib_send.at[number, place]).start()

    def forward(number, word, chunk):
        for edge in range(4):
            block = field(word, edge)

            @pl.when(block < CHIPS)
            def _():
                edge_copy(edge, block, chunk, send_sem.at[number, edge]).start()

    for chunk in range(CHUNKS):
        forward(0, outs[0], chunk)
    for chunk in range(CHUNKS):
        sib_copy(chip, chunk, sib_send.at[ROUNDS, 0]).start()

    def load_keys(block):
        both = kv[pl.ds(2 * block, 2), :, 0].reshape(2 * ROWS, DH)
        return jnp.concatenate([both, far[block]], axis=1)

    def load_values(block):
        both = kv[pl.ds(2 * block, 2), :, 1].reshape(2 * ROWS, DH)
        return jnp.concatenate([both, jnp.ones_like(both)], axis=1)

    def load_queries(h):
        return jnp.concatenate([q_ref[:, pl.ds(pl.multiple_of(h * DH, DH), DH)], mine[...]], axis=1)

    def wide(x, count):
        return jnp.concatenate([x] * count, axis=1)

    load_q.wait()
    sib_whole(chip, sib_send.at[ROUNDS, 0]).wait_recv()

    @pl.loop(0, 2)
    def _(half):
        keys, values = load_keys(chip), load_values(chip)
        shape = (ROWS, 2 * ROWS)
        key_pos = lax.broadcasted_iota(jnp.int32, shape, 1)
        causal = key_pos <= core * ROWS + lax.broadcasted_iota(jnp.int32, shape, 0)
        for i in range(HQ // 2):
            h = half * (HQ // 2) + i
            scores = lax.dot_general(load_queries(h), keys, NT, preferred_element_type=jnp.float32)
            scores = jnp.where(causal, scores, -1e30)
            peak = jnp.broadcast_to(jnp.max(scores, axis=1, keepdims=True), (ROWS, DH))
            top[h] = peak
            weights = jnp.exp2((scores - wide(peak, 4)) * SCALE).astype(jnp.bfloat16)
            acc[h] = jnp.dot(weights, values, preferred_element_type=jnp.float32)

    for chunk in range(CHUNKS):
        receive(0, ins[0], chunk)
        forward(1, outs[1], chunk)

    def absorb(blocks, half):
        count = len(blocks)
        keys = jnp.concatenate([load_keys(b) for b in blocks], axis=0)
        values = jnp.concatenate([load_values(b) for b in blocks], axis=0)
        number = HQ // 2
        kept = {}
        for step in range(number + 1):
            if step < number:
                h = half * number + step
                scores = lax.dot_general(load_queries(h), keys, NT, preferred_element_type=jnp.float32)
                old = top[h]
                new = jnp.maximum(old, jnp.max(scores, axis=1, keepdims=True))
                top[h] = new
                fade = jnp.exp2((old - new) * SCALE)
                weights = jnp.exp2((scores - wide(new, 4 * count)) * SCALE).astype(jnp.bfloat16)
                kept[step] = (fade, weights)
            if step >= 1:
                h = half * number + step - 1
                fade, weights = kept.pop(step - 1)
                acc[h] = acc[h] * wide(fade, 2) + jnp.dot(
                    weights, values, preferred_element_type=jnp.float32
                )

    @pl.loop(0, 2 * ROUNDS)
    def _(step):
        number, half = step // 2, step % 2
        arrived = pick(ins, number + 1, 32767)
        leaving = pick(outs, number + 2, 1048575)
        for i in range(CHUNKS // 2):
            chunk = half * (CHUNKS // 2) + i
            receive(number + 1, arrived, chunk)
            forward(number + 2, leaving, chunk)

        word = pick(ins, number, 32767)
        needed = word // 32768
        blocks = [field(word, place) for place in range(3)]

        @pl.when(half == 0)
        def _():
            for place in range(3):
                @pl.when(place < needed)
                def _():
                    sib_whole(blocks[place], sib_send.at[0, 0]).wait_recv()

        for count in range(1, 4):
            @pl.when(needed == count)
            def _():
                absorb(blocks[:count], half)

    for h in range(HQ):
        out_ref[:, h * DH:(h + 1) * DH] = (acc[h, :, :DH] / acc[h, :, DH:]).astype(jnp.bfloat16)

    sib_whole(chip, sib_send.at[ROUNDS, 0]).wait_send()
    for number in range(ROUNDS):
        for place in range(3):
            @pl.when(place < ins[number] // 32768)
            def _():
                sib_whole(chip, sib_send.at[number, place]).wait_send()
        for edge in range(4):
            block = field(outs[number], edge)

            @pl.when(block < CHIPS)
            def _():
                sib_whole(chip, send_sem.at[number, edge]).wait_send()


def local(queries, keys, values, lengths):
    anywhere = pl.BlockSpec(memory_space=pl.ANY)
    return pl.pallas_call(
        kernel,
        out_shape=jax.ShapeDtypeStruct(queries.shape, jnp.bfloat16),
        in_specs=[anywhere] * 3 + [pl.BlockSpec(memory_space=pltpu.SMEM)],
        out_specs=pl.BlockSpec(memory_space=pltpu.VMEM),
        scratch_shapes=[
            pltpu.VMEM((ROWS, HQ * DH), jnp.bfloat16),
            pltpu.VMEM((2 * CHIPS, CHUNKS, 2, PART, DH), jnp.bfloat16),
            pltpu.VMEM((CHIPS, 2 * ROWS, DH), jnp.bfloat16),
            pltpu.VMEM((ROWS, DH), jnp.bfloat16),
            pltpu.VMEM((HQ, ROWS, DH), jnp.float32),
            pltpu.VMEM((HQ, ROWS, 2 * DH), jnp.float32),
            pltpu.SemaphoreType.DMA,
            pltpu.SemaphoreType.DMA,
            pltpu.SemaphoreType.DMA((CHIPS, CHUNKS)),
            pltpu.SemaphoreType.DMA((CHIPS,)),
            pltpu.SemaphoreType.DMA((ROUNDS, 4)),
            pltpu.SemaphoreType.DMA((ROUNDS + 1, 3)),
        ],
        compiler_params=pltpu.CompilerParams(
            collective_id=0, has_side_effects=True, vmem_limit_bytes=56 * 2**20
        ),
    )(queries, keys, values, lengths)


def solution(mesh):
    placed = (P("seq", "head"), P("seq", "head"), P("seq", "head"), P())
    return jax.shard_map(
        local, mesh=mesh, in_specs=placed, out_specs=P("seq", "head"), check_vma=False
    )
```

```python
import math

import jax
import jax.numpy as jnp
from jax import lax
from jax.experimental import pallas as pl
from jax.experimental.pallas import tpu as pltpu
from jax.sharding import PartitionSpec as P

MESH = pl.DeviceIdType.MESH
HQ = 8
DH = 128
NDOC = 16
ROWS = 256
CHIPS = 16
HALF = ROWS // 2
FAR = -(2.0**20)
SCALE = math.log2(math.e) / math.sqrt(DH)
REACH = 9
LIMIT = 2.0**100
PIECE = 64

FIRST = 3
WORK_WORDS = (
    (0, 0, 32771, 32772, 32774, 32777, 65856, 32780, 32768, 65616, 65683, 65748, 65846, 65880, 66384, 66044),
    (0, 0, 32770, 32773, 0, 32775, 0, 32770, 32769, 32785, 32773, 65778, 32791, 0, 66348, 66482),
    (0, 32768, 0, 0, 32773, 32776, 32769, 32779, 0, 65637, 32785, 0, 66221, 65913, 66091, 66413),
    (0, 32769, 0, 32771, 32775, 32768, 0, 32777, 65667, 65728, 66054, 66154, 66184, 66070, 66221, 32782),
    (0, 0, 0, 32770, 0, 32772, 65763, 32778, 65996, 65761, 65993, 66212, 65930, 66280, 65880, 66067),
    (0, 0, 32768, 0, 32772, 32769, 65605, 65574, 66018, 65679, 65810, 65705, 66002, 66124, 66043, 66362),
    (0, 0, 0, 32769, 65539, 32773, 32779, 65677, 65704, 65832, 65763, 65969, 65739, 65967, 66254, 66092),
    (0, 0, 32769, 0, 32770, 65638, 65832, 65768, 65901, 65870, 65922, 66056, 65779, 66101, 66290, 66197),
    (0, 0, 0, 32768, 32769, 32770, 65732, 65699, 65830, 65933, 65898, 65900, 66096, 66153, 66195, 66264),
    (0, 0, 0, 0, 0, 0, 0, 32768, 65863, 32779, 65967, 66030, 32783, 66190, 0, 32791),
)
IN_WORDS = (
    (32771, 118214, 163843, 252164, 196998, 163849, 328000, 163852, 197280, 327760, 327827, 327892, 327990, 328024, 504656, 328188),
    (0, 32783, 196866, 163845, 0, 163847, 32782, 163842, 163841, 197265, 163845, 327922, 163863, 0, 163865, 328626),
    (0, 196736, 0, 0, 163845, 197032, 163841, 163851, 32788, 327781, 163857, 0, 500397, 328057, 505387, 506733),
    (0, 197313, 0, 196963, 163847, 163840, 0, 163849, 503939, 327872, 501254, 496234, 504148, 328214, 502549, 0),
    (0, 32780, 0, 163842, 0, 163844, 327907, 163850, 506958, 507105, 500302, 496949, 163858, 504552, 506363, 518675),
    (0, 0, 163840, 0, 163844, 163841, 502853, 504870, 505000, 163844, 493795, 500145, 498030, 505330, 0, 360857),
    (0, 0, 0, 163841, 327683, 163845, 0, 327940, 327883, 506152, 328012, 503184, 327923, 501301, 328278, 328369),
    (0, 0, 163841, 0, 163842, 327782, 327976, 163847, 0, 504234, 328171, 163854, 163856, 328147, 328311, 328468),
    (0, 0, 0, 163840, 163841, 163842, 327876, 491683, 327913, 0, 163853, 163855, 328177, 163860, 163860, 328438),
    (0, 0, 0, 0, 0, 0, 0, 0, 163850, 163851, 0, 0, 0, 0, 0, 0),
)
OUT_WORDS = (
    (268550144, 461915747, 268552292, 462949478, 463753321, 268555370, 464525420, 268557966, 268443760, 268559987, 268446324, 268561526, 134217848, 134217850, 134217852, 0),
    (134217953, 268436578, 454412901, 268553863, 134217736, 134217995, 268524301, 268508718, 134217841, 268444818, 134217780, 134217847, 134217881, 0, 134217853, 0),
    (268436064, 268535523, 268503588, 134217926, 268554344, 447338123, 268556845, 134217966, 268444305, 0, 268445845, 0, 134217849, 134217883, 0, 0),
    (134217825, 449715430, 134217827, 462433383, 268570860, 268441225, 268555296, 134217998, 268446304, 134217840, 268437619, 134217844, 268440182, 268457080, 268507184, 0),
    (134217731, 134217967, 446812258, 268552836, 0, 134217831, 448388202, 134217868, 268460129, 268452978, 134217845, 268439154, 268456567, 134217851, 268458106, 268459631),
    (0, 268438624, 268538082, 268554340, 268553349, 134217965, 268452449, 472766498, 134217760, 268454499, 268454001, 268510247, 134217773, 134217771, 268555897, 464789101),
    (0, 465045633, 0, 455988835, 268553829, 463802400, 0, 0, 268507185, 134217766, 268456560, 268457075, 268458101, 134217846, 268460661, 134217778),
    (0, 450484321, 0, 134217826, 134217830, 134217832, 268453479, 268571177, 0, 268445807, 134217838, 268440723, 0, 268460151, 268459128, 268507699),
    (0, 134217731, 134217824, 134217899, 0, 268452452, 268452965, 268571686, 134217748, 268508711, 0, 268458609, 134217844, 268512815, 0, 134217952),
)
EDGES = ((-2, 0), (-2, 1), (-1, 0), (-1, 1), (0, 1), (1, 0), (1, 1), (2, 0))

NT = (((1,), (1,)), ((), ()))


def pick(table, index, default):
    value = jnp.int32(default)
    for number, entry in enumerate(table):
        value = jnp.where(index == number, entry, value)
    return value


def kernel(
    queries_hbm, keys_hbm, values_hbm, lengths_hbm, out_hbm, over_hbm, gathered_hbm,
    out_ref, over_ref, q_ref, kv, far, mine, acc, lengths_ref,
    q_sem, own_sem, lengths_sem, recv_sem, sib_recv, send_sem, sib_send, keep_sem, out_sem,
):
    seq, head = lax.axis_index("seq"), lax.axis_index("head")
    core = seq % 2
    chip = seq // 2
    z = chip % 8
    high = chip // 8
    own = 2 * chip + core

    def device(flip, move, core):
        side = high + flip - 2 * high * flip
        return (side * 16 + ((z + move + 8) % 8) * 2 + core, head)

    sibling = device(0, 0, 1 - core)
    barrier = pltpu.get_barrier_semaphore()
    partners = sorted({(m, f) for m, f in EDGES} | {(-m, f) for m, f in EDGES})
    for move, flip in partners:
        pl.semaphore_signal(barrier, inc=1, device_id=device(flip, move, core), device_id_type=MESH)
    pl.semaphore_signal(barrier, inc=1, device_id=sibling, device_id_type=MESH)

    load_lengths = pltpu.make_async_copy(lengths_hbm, lengths_ref, lengths_sem)
    load_lengths.start()
    for half in range(2):
        part = pl.ds(half * HALF, HALF)
        pltpu.make_async_copy(keys_hbm.at[part], kv.at[own, half, 0], own_sem).start()
        pltpu.make_async_copy(values_hbm.at[part], kv.at[own, half, 1], own_sem).start()
    load_q = pltpu.make_async_copy(queries_hbm, q_ref, q_sem)
    load_q.start()

    ins = [pick(row, chip, 0) for row in IN_WORDS]
    outs = [pick(row, chip, 0) for row in OUT_WORDS]
    works = [pick(row, chip, 0) for row in WORK_WORDS]

    load_lengths.wait()
    lane = lax.broadcasted_iota(jnp.int32, (1, DH), 1)
    first = jnp.zeros((1, DH), jnp.int32)
    last = jnp.zeros((1, DH), jnp.int32)
    begin = jnp.int32(0)
    for number in range(NDOC):
        end = begin + lengths_ref[number]
        first = jnp.where(lane == number, begin, first)
        last = jnp.where(lane == number, end, last)
        begin = end
    row_pos = own * ROWS + lax.broadcasted_iota(jnp.int32, (ROWS, DH), 0)
    mark = ((row_pos >= first) & (row_pos < last)).astype(jnp.float32)
    mine[0] = mark.astype(jnp.bfloat16)
    low = jnp.where(lane < NDOC, first, 0)
    top_pos = jnp.where(lane < NDOC, last, 2 * ROWS * CHIPS)

    @pl.loop(jnp.maximum(chip - REACH, 0), chip + 1)
    def _(block):
        for side in range(2):
            for half in range(2):
                at = block * 2 * ROWS + side * ROWS + half * HALF
                pos = at + lax.broadcasted_iota(jnp.int32, (HALF, DH), 0)
                inside = (pos >= low) & (pos < top_pos)
                away = jnp.where(inside, (lane == NDOC).astype(jnp.float32), FAR)
                far[block, half, side] = away.astype(jnp.bfloat16)

    pltpu.make_async_copy(kv.at[own], kv.at[own], own_sem).wait()
    pl.semaphore_wait(barrier, len(partners) + 1)

    def sib_copy(item, side, sem):
        part = kv.at[2 * (item // 2) + side, item % 2]
        return pltpu.make_async_remote_copy(
            src_ref=part, dst_ref=part, send_sem=sem, recv_sem=sib_recv.at[item],
            device_id=sibling, device_id_type=MESH,
        )

    def edge_copy(item, target, sem):
        part = kv.at[2 * (item // 2) + core, item % 2]
        return pltpu.make_async_remote_copy(
            src_ref=part, dst_ref=part, send_sem=sem, recv_sem=recv_sem.at[item],
            device_id=target, device_id_type=MESH,
        )

    def receive(step, word):
        arrive, needed = (word // 2**15) % 4, word // 2**17
        for place in range(3):
            item = (word // 32**place) % 32

            @pl.when(place < arrive)
            def _():
                edge_copy(item, sibling, send_sem.at[0, 0]).wait_recv()

            @pl.when(place < needed)
            def _():
                sib_copy(item, core, sib_send.at[item]).start()

    def forward(step, word):
        for place in range(3):
            entry = (word // 512**place) % 512
            edge = entry // 32

            @pl.when(place < word // 512**3)
            def _():
                target = device(edge // 5, edge % 5 - 2, core)
                edge_copy(entry % 32, target, send_sem.at[step, place]).start()

    def keep(item, sem):
        at = (pl.ds(2 * (item // 2), 2), item % 2)
        return pltpu.make_async_copy(kv.at[at], gathered_hbm.at[at], sem)

    def settle(step, word):
        for place in range(3):
            @pl.when(place < word // 512**3)
            def _():
                edge_copy(own, sibling, send_sem.at[step, place]).wait_send()

    for step in range(FIRST):
        forward(step, outs[step])
    for half in range(2):
        sib_copy(2 * chip + half, core, sib_send.at[2 * chip + half]).start()

    def load_keys(item):
        both = kv[pl.ds(2 * (item // 2), 2), item % 2, 0].reshape(ROWS, DH)
        away = far[item // 2, item % 2].reshape(ROWS, DH)
        return jnp.concatenate([both, away], axis=1)

    def load_values(item):
        both = kv[pl.ds(2 * (item // 2), 2), item % 2, 1].reshape(ROWS, DH)
        return jnp.concatenate([both, jnp.ones_like(both)], axis=1)

    def load_queries(h, which):
        return jnp.concatenate([q_ref[:, h * DH:(h + 1) * DH], mine[which]], axis=1)

    def product(h, which, keys):
        return lax.dot_general(load_queries(h, which), keys, NT, preferred_element_type=jnp.float32)

    def absorb(items):
        keys = jnp.concatenate([load_keys(item) for item in items], axis=0)
        values = jnp.concatenate([load_values(item) for item in items], axis=0)
        weights = None
        for h in range(HQ + 1):
            ready = weights
            if h < HQ:
                weights = jnp.exp2(product(h, h + 1, keys) * SCALE).astype(jnp.bfloat16)
            if h >= 1:
                acc[h - 1] += jnp.dot(ready, values, preferred_element_type=jnp.float32)

    load_q.wait()
    for half in range(2):
        sib_copy(2 * chip + half, 1 - core, sib_send.at[0]).wait_recv()
    shape = (ROWS, 2 * ROWS)
    column = lax.broadcasted_iota(jnp.int32, shape, 1)
    column = (column // ROWS) * HALF + ((column // HALF) % 2) * ROWS + column % HALF
    causal = column <= core * ROWS + lax.broadcasted_iota(jnp.int32, shape, 0)
    items = [2 * chip, 2 * chip + 1]
    for half in range(2):
        keep(items[half], keep_sem.at[items[half]]).start()
    keys = jnp.concatenate([load_keys(item) for item in items], axis=0)
    values = jnp.concatenate([load_values(item) for item in items], axis=0)
    for h in range(HQ):
        scores = jnp.where(causal, product(h, 0, keys), -1e30)
        shift = jnp.max(scores, axis=1, keepdims=True).astype(jnp.bfloat16).astype(jnp.float32)
        mine[h + 1] = jnp.where(lane == NDOC, -shift, mark).astype(jnp.bfloat16)
        weights = jnp.exp2((scores - shift) * SCALE).astype(jnp.bfloat16)
        acc[h] = jnp.dot(weights, values, preferred_element_type=jnp.float32)

    @pl.loop(FIRST, FIRST + 1 + len(WORK_WORDS))
    def _(step):
        arrived = pick(ins, step - FIRST, 0)
        receive(step, arrived)
        forward(step, pick(outs, step, 0))

        word = pick(works, step - 1 - FIRST, 0)
        needed = word // 2**15
        items = [(word // 32**place) % 32 for place in range(3)]
        for place in range(3):
            @pl.when(place < needed)
            def _():
                sib_copy(items[place], 1 - core, sib_send.at[0]).wait_recv()
                keep(items[place], keep_sem.at[items[place]]).start()

        for count in range(1, 4):
            @pl.when(needed == count)
            def _():
                absorb(items[:count])

    def store(h):
        at = (slice(None), pl.ds(h * DH, DH))
        return pltpu.make_async_copy(out_ref.at[at], out_hbm.at[at], out_sem.at[h])

    over = jnp.zeros((ROWS, DH), jnp.float32)
    for h in range(HQ):
        total = acc[h, :, DH:]
        over = jnp.where(total < LIMIT, over, 1.0)
        out_ref[:, h * DH:(h + 1) * DH] = (acc[h, :, :DH] / total).astype(jnp.bfloat16)
        store(h).start()
    over_ref[...] = jnp.max(over.reshape(ROWS // 8, 8, DH), axis=0)
    store_over = pltpu.make_async_copy(over_ref, over_hbm, out_sem.at[HQ])
    store_over.start()

    @pl.loop(2 * jnp.maximum(chip - REACH, 0), 2 * chip + 2)
    def _(item):
        sib_copy(own, core, sib_send.at[item]).wait_send()
        keep(own, keep_sem.at[item]).wait()

    @pl.loop(0, len(OUT_WORDS))
    def _(step):
        settle(step, pick(outs, step, 0))

    for h in range(HQ):
        store(h).wait()
    store_over.wait()


def repair(
    attended_hbm, over_hbm, gathered_hbm, queries_hbm, lengths_hbm, out_hbm,
    over_ref, kv, q_ref, o_ref, top, acc, lengths_ref, sem, over_sem, in_sem, out_sem,
):
    load = pltpu.make_async_copy(over_hbm, over_ref, over_sem)
    load.start()
    def fetch(piece):
        at = pl.ds(piece * PIECE, PIECE)
        return pltpu.make_async_copy(attended_hbm.at[at], o_ref.at[at], in_sem.at[piece])

    def store(piece):
        at = pl.ds(piece * PIECE, PIECE)
        return pltpu.make_async_copy(o_ref.at[at], out_hbm.at[at], out_sem.at[piece])

    for piece in range(ROWS // PIECE):
        fetch(piece).start()
    for piece in range(ROWS // PIECE):
        fetch(piece).wait()
        store(piece).start()
    load.wait()
    over = jnp.max(over_ref[...])
    for piece in range(ROWS // PIECE):
        store(piece).wait()

    @pl.when(over > 0.0)
    def _():
        seq = lax.axis_index("seq")
        chip = seq // 2
        load = pltpu.make_async_copy(gathered_hbm, kv, sem)
        load.start()
        load.wait()
        load = pltpu.make_async_copy(queries_hbm, q_ref, sem)
        load.start()
        load.wait()
        load = pltpu.make_async_copy(lengths_hbm, lengths_ref, sem)
        load.start()
        load.wait()
        shape = (ROWS, ROWS)
        row = seq * ROWS + lax.broadcasted_iota(jnp.int32, shape, 0)
        low = jnp.zeros(shape, jnp.int32)
        begin = jnp.int32(0)
        for number in range(NDOC):
            low = jnp.where(row >= begin, begin, low)
            begin = begin + lengths_ref[number]
        top[...] = jnp.full_like(top, -1e30)
        acc[...] = jnp.zeros_like(acc)

        @pl.loop(2 * jnp.maximum(chip - REACH, 0), seq + 1)
        def _(block):
            key = block * ROWS + lax.broadcasted_iota(jnp.int32, shape, 1)
            allowed = (key >= low) & (key <= row)
            keys = kv[block, :, 0].reshape(ROWS, DH)
            values = kv[block, :, 1].reshape(ROWS, DH)
            values = jnp.concatenate([values, jnp.ones_like(values)], axis=1)
            for h in range(HQ):
                queries = q_ref[:, h * DH:(h + 1) * DH]
                scores = lax.dot_general(queries, keys, NT, preferred_element_type=jnp.float32)
                old = top[h]
                peak = jnp.max(jnp.where(allowed, scores, -1e30), axis=1, keepdims=True)
                new = jnp.maximum(old, peak)
                top[h] = new
                fade = jnp.exp2((old - new) * SCALE)
                both = jnp.concatenate([new, new], axis=1)
                weights = jnp.where(allowed, jnp.exp2((scores - both) * SCALE), 0.0)
                acc[h] = acc[h] * jnp.concatenate([fade, fade], axis=1) + jnp.dot(
                    weights.astype(jnp.bfloat16), values, preferred_element_type=jnp.float32
                )

        for h in range(HQ):
            o_ref[:, h * DH:(h + 1) * DH] = (acc[h, :, :DH] / acc[h, :, DH:]).astype(jnp.bfloat16)
        again = pltpu.make_async_copy(o_ref, out_hbm, sem)
        again.start()
        again.wait()


def local(queries, keys, values, lengths):
    far_away = pl.BlockSpec(memory_space=pltpu.HBM)
    attended, over, gathered = pl.pallas_call(
        kernel,
        out_shape=(
            jax.ShapeDtypeStruct(queries.shape, jnp.bfloat16),
            jax.ShapeDtypeStruct((8, DH), jnp.float32),
            jax.ShapeDtypeStruct((2 * CHIPS, 2, 2, HALF, DH), jnp.bfloat16),
        ),
        in_specs=[far_away] * 4,
        out_specs=(far_away,) * 3,
        scratch_shapes=[
            pltpu.VMEM((ROWS, HQ * DH), jnp.bfloat16),
            pltpu.VMEM((8, DH), jnp.float32),
            pltpu.VMEM((ROWS, HQ * DH), jnp.bfloat16),
            pltpu.VMEM((2 * CHIPS, 2, 2, HALF, DH), jnp.bfloat16),
            pltpu.VMEM((CHIPS, 2, 2, HALF, DH), jnp.bfloat16),
            pltpu.VMEM((HQ + 1, ROWS, DH), jnp.bfloat16),
            pltpu.VMEM((HQ, ROWS, 2 * DH), jnp.float32),
            pltpu.SMEM((NDOC,), jnp.int32),
            pltpu.SemaphoreType.DMA,
            pltpu.SemaphoreType.DMA,
            pltpu.SemaphoreType.DMA,
            pltpu.SemaphoreType.DMA((2 * CHIPS,)),
            pltpu.SemaphoreType.DMA((2 * CHIPS,)),
            pltpu.SemaphoreType.DMA((len(OUT_WORDS), 3)),
            pltpu.SemaphoreType.DMA((2 * CHIPS,)),
            pltpu.SemaphoreType.DMA((2 * CHIPS,)),
            pltpu.SemaphoreType.DMA((HQ + 1,)),
        ],
        compiler_params=pltpu.CompilerParams(
            collective_id=0, has_side_effects=True, vmem_limit_bytes=60 * 2**20
        ),
    )(queries, keys, values, lengths)
    return pl.pallas_call(
        repair,
        out_shape=jax.ShapeDtypeStruct(queries.shape, jnp.bfloat16),
        in_specs=[far_away] * 5,
        out_specs=far_away,
        scratch_shapes=[
            pltpu.VMEM((8, DH), jnp.float32),
            pltpu.VMEM((2 * CHIPS, 2, 2, HALF, DH), jnp.bfloat16),
            pltpu.VMEM((ROWS, HQ * DH), jnp.bfloat16),
            pltpu.VMEM((ROWS, HQ * DH), jnp.bfloat16),
            pltpu.VMEM((HQ, ROWS, DH), jnp.float32),
            pltpu.VMEM((HQ, ROWS, 2 * DH), jnp.float32),
            pltpu.SMEM((NDOC,), jnp.int32),
            pltpu.SemaphoreType.DMA,
            pltpu.SemaphoreType.DMA,
            pltpu.SemaphoreType.DMA((ROWS // PIECE,)),
            pltpu.SemaphoreType.DMA((ROWS // PIECE,)),
        ],
        compiler_params=pltpu.CompilerParams(vmem_limit_bytes=60 * 2**20),
    )(attended, over, gathered, queries, lengths)


def solution(mesh):
    placed = (P("seq", "head"), P("seq", "head"), P("seq", "head"), P())
    return jax.shard_map(
        local, mesh=mesh, in_specs=placed, out_specs=P("seq", "head"), check_vma=False
    )
```

```python
import math

import jax
import jax.numpy as jnp
from jax import lax
from jax.experimental import pallas as pl
from jax.experimental.pallas import tpu as pltpu
from jax.sharding import PartitionSpec as P

MESH = pl.DeviceIdType.MESH
HQ = 8
DH = 128
NDOC = 16
ROWS = 256
CHIPS = 16
HALF = ROWS // 2
FAR = -(2.0**20)
SCALE = math.log2(math.e) / math.sqrt(DH)
REACH = 9
BEHIND = 4
LIMIT = 2.0**100

FIRST = 3
WORK_WORDS = (
    (0, 0, 32771, 32772, 32774, 32777, 65856, 32780, 32768, 65616, 65683, 65748, 65846, 65880, 66384, 66044),
    (0, 0, 32770, 32773, 0, 32775, 0, 32770, 32769, 32785, 32773, 65778, 32791, 0, 66348, 66482),
    (0, 32768, 0, 0, 32773, 32776, 32769, 32779, 0, 65637, 32785, 0, 66221, 65913, 66091, 66413),
    (0, 32769, 0, 32771, 32775, 32768, 0, 32777, 65667, 65728, 66054, 66154, 66184, 66070, 66221, 32782),
    (0, 0, 0, 32770, 0, 32772, 65763, 32778, 65996, 65761, 65993, 66212, 65930, 66280, 65880, 66067),
    (0, 0, 32768, 0, 32772, 32769, 65605, 65574, 66018, 65679, 65810, 65705, 66002, 66124, 66043, 66362),
    (0, 0, 0, 32769, 65539, 32773, 32779, 65677, 65704, 65832, 65763, 65969, 65739, 65967, 66254, 66092),
    (0, 0, 32769, 0, 32770, 65638, 65832, 65768, 65901, 65870, 65922, 66056, 65779, 66101, 66290, 66197),
    (0, 0, 0, 32768, 32769, 32770, 65732, 65699, 65830, 65933, 65898, 65900, 66096, 66153, 66195, 66264),
    (0, 0, 0, 0, 0, 0, 0, 32768, 65863, 32779, 65967, 66030, 32783, 66190, 0, 32791),
)
IN_WORDS = (
    (32771, 118214, 163843, 252164, 196998, 163849, 328000, 163852, 197280, 327760, 327827, 327892, 327990, 328024, 504656, 328188),
    (0, 32783, 196866, 163845, 0, 163847, 32782, 163842, 163841, 197265, 163845, 327922, 163863, 0, 163865, 328626),
    (0, 196736, 0, 0, 163845, 197032, 163841, 163851, 32788, 327781, 163857, 0, 500397, 328057, 505387, 506733),
    (0, 197313, 0, 196963, 163847, 163840, 0, 163849, 503939, 327872, 501254, 496234, 504148, 328214, 502549, 0),
    (0, 32780, 0, 163842, 0, 163844, 327907, 163850, 506958, 507105, 500302, 496949, 163858, 504552, 506363, 518675),
    (0, 0, 163840, 0, 163844, 163841, 502853, 504870, 505000, 163844, 493795, 500145, 498030, 505330, 0, 360857),
    (0, 0, 0, 163841, 327683, 163845, 0, 327940, 327883, 506152, 328012, 503184, 327923, 501301, 328278, 328369),
    (0, 0, 163841, 0, 163842, 327782, 327976, 163847, 0, 504234, 328171, 163854, 163856, 328147, 328311, 328468),
    (0, 0, 0, 163840, 163841, 163842, 327876, 491683, 327913, 0, 163853, 163855, 328177, 163860, 163860, 328438),
    (0, 0, 0, 0, 0, 0, 0, 0, 163850, 163851, 0, 0, 0, 0, 0, 0),
)
OUT_WORDS = (
    (268550144, 461915747, 268552292, 462949478, 463753321, 268555370, 464525420, 268557966, 268443760, 268559987, 268446324, 268561526, 134217848, 134217850, 134217852, 0),
    (134217953, 268436578, 454412901, 268553863, 134217736, 134217995, 268524301, 268508718, 134217841, 268444818, 134217780, 134217847, 134217881, 0, 134217853, 0),
    (268436064, 268535523, 268503588, 134217926, 268554344, 447338123, 268556845, 134217966, 268444305, 0, 268445845, 0, 134217849, 134217883, 0, 0),
    (134217825, 449715430, 134217827, 462433383, 268570860, 268441225, 268555296, 134217998, 268446304, 134217840, 268437619, 134217844, 268440182, 268457080, 268507184, 0),
    (134217731, 134217967, 446812258, 268552836, 0, 134217831, 448388202, 134217868, 268460129, 268452978, 134217845, 268439154, 268456567, 134217851, 268458106, 268459631),
    (0, 268438624, 268538082, 268554340, 268553349, 134217965, 268452449, 472766498, 134217760, 268454499, 268454001, 268510247, 134217773, 134217771, 268555897, 464789101),
    (0, 465045633, 0, 455988835, 268553829, 463802400, 0, 0, 268507185, 134217766, 268456560, 268457075, 268458101, 134217846, 268460661, 134217778),
    (0, 450484321, 0, 134217826, 134217830, 134217832, 268453479, 268571177, 0, 268445807, 134217838, 268440723, 0, 268460151, 268459128, 268507699),
    (0, 134217731, 134217824, 134217899, 0, 268452452, 268452965, 268571686, 134217748, 268508711, 0, 268458609, 134217844, 268512815, 0, 134217952),
)
EDGES = ((-2, 0), (-2, 1), (-1, 0), (-1, 1), (0, 1), (1, 0), (1, 1), (2, 0))

NT = (((1,), (1,)), ((), ()))


def pick(table, index, default):
    value = jnp.int32(default)
    for number, entry in enumerate(table):
        value = jnp.where(index == number, entry, value)
    return value


def kernel(
    queries_hbm, keys_hbm, values_hbm, lengths_hbm, out_ref, over_ref, gathered_hbm,
    q_ref, kv, far, mine, acc, lengths_ref,
    q_sem, own_sem, lengths_sem, recv_sem, sib_recv, send_sem, sib_send, keep_sem,
):
    seq, head = lax.axis_index("seq"), lax.axis_index("head")
    core = seq % 2
    chip = seq // 2
    z = chip % 8
    high = chip // 8
    own = 2 * chip + core

    def device(flip, move, core):
        side = high + flip - 2 * high * flip
        return (side * 16 + ((z + move + 8) % 8) * 2 + core, head)

    sibling = device(0, 0, 1 - core)
    barrier = pltpu.get_barrier_semaphore()
    partners = sorted({(m, f) for m, f in EDGES} | {(-m, f) for m, f in EDGES})
    for move, flip in partners:
        pl.semaphore_signal(barrier, inc=1, device_id=device(flip, move, core), device_id_type=MESH)
    pl.semaphore_signal(barrier, inc=1, device_id=sibling, device_id_type=MESH)

    load_lengths = pltpu.make_async_copy(lengths_hbm, lengths_ref, lengths_sem)
    load_lengths.start()
    for half in range(2):
        part = pl.ds(half * HALF, HALF)
        pltpu.make_async_copy(keys_hbm.at[part], kv.at[own, half, 0], own_sem).start()
        pltpu.make_async_copy(values_hbm.at[part], kv.at[own, half, 1], own_sem).start()
    load_q = pltpu.make_async_copy(queries_hbm, q_ref, q_sem)
    load_q.start()

    ins = [pick(row, chip, 0) for row in IN_WORDS]
    outs = [pick(row, chip, 0) for row in OUT_WORDS]
    works = [pick(row, chip, 0) for row in WORK_WORDS]

    load_lengths.wait()
    lane = lax.broadcasted_iota(jnp.int32, (1, DH), 1)
    first = jnp.zeros((1, DH), jnp.int32)
    last = jnp.zeros((1, DH), jnp.int32)
    begin = jnp.int32(0)
    for number in range(NDOC):
        end = begin + lengths_ref[number]
        first = jnp.where(lane == number, begin, first)
        last = jnp.where(lane == number, end, last)
        begin = end
    row_pos = own * ROWS + lax.broadcasted_iota(jnp.int32, (ROWS, DH), 0)
    mark = ((row_pos >= first) & (row_pos < last)).astype(jnp.float32)
    mine[0] = mark.astype(jnp.bfloat16)
    low = jnp.where(lane < NDOC, first, 0)
    top_pos = jnp.where(lane < NDOC, last, 2 * ROWS * CHIPS)

    @pl.loop(jnp.maximum(chip - REACH, 0), chip + 1)
    def _(block):
        for side in range(2):
            for half in range(2):
                at = block * 2 * ROWS + side * ROWS + half * HALF
                pos = at + lax.broadcasted_iota(jnp.int32, (HALF, DH), 0)
                inside = (pos >= low) & (pos < top_pos)
                away = jnp.where(inside, (lane == NDOC).astype(jnp.float32), FAR)
                far[block, half, side] = away.astype(jnp.bfloat16)

    pltpu.make_async_copy(kv.at[own], kv.at[own], own_sem).wait()
    pl.semaphore_wait(barrier, len(partners) + 1)

    def sib_copy(item, side, sem):
        part = kv.at[2 * (item // 2) + side, item % 2]
        return pltpu.make_async_remote_copy(
            src_ref=part, dst_ref=part, send_sem=sem, recv_sem=sib_recv.at[item],
            device_id=sibling, device_id_type=MESH,
        )

    def edge_copy(item, target, sem):
        part = kv.at[2 * (item // 2) + core, item % 2]
        return pltpu.make_async_remote_copy(
            src_ref=part, dst_ref=part, send_sem=sem, recv_sem=recv_sem.at[item],
            device_id=target, device_id_type=MESH,
        )

    def receive(step, word):
        arrive, needed = (word // 2**15) % 4, word // 2**17
        for place in range(3):
            item = (word // 32**place) % 32

            @pl.when(place < arrive)
            def _():
                edge_copy(item, sibling, send_sem.at[0, 0]).wait_recv()

            @pl.when(place < needed)
            def _():
                sib_copy(item, core, sib_send).start()

    def forward(step, word):
        for place in range(3):
            entry = (word // 512**place) % 512
            edge = entry // 32

            @pl.when(place < word // 512**3)
            def _():
                target = device(edge // 5, edge % 5 - 2, core)
                edge_copy(entry % 32, target, send_sem.at[step, place]).start()

    def keep(item, sem):
        at = (pl.ds(2 * (item // 2), 2), item % 2)
        return pltpu.make_async_copy(kv.at[at], gathered_hbm.at[at], sem)

    def settle(step, word):
        for place in range(3):
            @pl.when(place < word // 512**3)
            def _():
                edge_copy(own, sibling, send_sem.at[step, place]).wait_send()

    for step in range(FIRST):
        forward(step, outs[step])
    for half in range(2):
        sib_copy(2 * chip + half, core, sib_send).start()

    def load_keys(item):
        both = kv[pl.ds(2 * (item // 2), 2), item % 2, 0].reshape(ROWS, DH)
        away = far[item // 2, item % 2].reshape(ROWS, DH)
        return jnp.concatenate([both, away], axis=1)

    def load_values(item):
        both = kv[pl.ds(2 * (item // 2), 2), item % 2, 1].reshape(ROWS, DH)
        return jnp.concatenate([both, jnp.ones_like(both)], axis=1)

    def load_queries(h, which):
        return jnp.concatenate([q_ref[:, h * DH:(h + 1) * DH], mine[which]], axis=1)

    def product(h, which, items):
        keys = jnp.concatenate([load_keys(item) for item in items], axis=0)
        return lax.dot_general(load_queries(h, which), keys, NT, preferred_element_type=jnp.float32)

    def mix(weights, items):
        values = jnp.concatenate([load_values(item) for item in items], axis=0)
        return jnp.dot(weights, values, preferred_element_type=jnp.float32)

    def absorb(items):
        weights = None
        for h in range(HQ + 1):
            ready = weights
            if h < HQ:
                weights = jnp.exp2(product(h, h + 1, items) * SCALE).astype(jnp.bfloat16)
            if h >= 1:
                acc[h - 1] += mix(ready, items)

    load_q.wait()
    for half in range(2):
        sib_copy(2 * chip + half, 1 - core, sib_send).wait_recv()
    shape = (ROWS, 2 * ROWS)
    column = lax.broadcasted_iota(jnp.int32, shape, 1)
    column = (column // ROWS) * HALF + ((column // HALF) % 2) * ROWS + column % HALF
    causal = column <= core * ROWS + lax.broadcasted_iota(jnp.int32, shape, 0)
    items = [2 * chip, 2 * chip + 1]
    for half in range(2):
        keep(items[half], keep_sem).start()
    for h in range(HQ):
        scores = jnp.where(causal, product(h, 0, items), -1e30)
        shift = jnp.max(scores, axis=1, keepdims=True).astype(jnp.bfloat16).astype(jnp.float32)
        mine[h + 1] = jnp.where(lane == NDOC, -shift, mark).astype(jnp.bfloat16)
        weights = jnp.exp2((scores - shift) * SCALE).astype(jnp.bfloat16)
        acc[h] = mix(weights, items)

    @pl.loop(FIRST, FIRST + 1 + len(WORK_WORDS))
    def _(step):
        arrived = pick(ins, step - FIRST, 0)
        receive(step, arrived)
        forward(step, pick(outs, step, 0))

        settle(step - BEHIND, pick(outs, step - BEHIND, 0))

        word = pick(works, step - 1 - FIRST, 0)
        needed = word // 2**15
        items = [(word // 32**place) % 32 for place in range(3)]
        for place in range(3):
            @pl.when(place < needed)
            def _():
                sib_copy(items[place], 1 - core, sib_send).wait_recv()
                keep(items[place], keep_sem).start()

        for count in range(1, 4):
            @pl.when(needed == count)
            def _():
                absorb(items[:count])

    over = jnp.zeros((ROWS, DH), jnp.float32)
    for h in range(HQ):
        total = acc[h, :, DH:]
        over = jnp.where(total < LIMIT, over, 1.0)
        out_ref[:, h * DH:(h + 1) * DH] = (acc[h, :, :DH] / total).astype(jnp.bfloat16)
    over_ref[...] = jnp.max(over.reshape(ROWS // 8, 8, DH), axis=0)

    for step in range(FIRST + 1 + len(WORK_WORDS) - BEHIND, len(OUT_WORDS)):
        settle(step, outs[step])

    for count in range(1, REACH + 2):
        @pl.when(jnp.minimum(chip, REACH) + 1 == count)
        def _():
            blocks = kv.at[pl.ds(0, count)]
            pltpu.make_async_remote_copy(
                src_ref=blocks, dst_ref=blocks, send_sem=sib_send, recv_sem=sib_recv.at[0],
                device_id=sibling, device_id_type=MESH,
            ).wait_send()
            kept = pl.ds(0, 2 * count)
            pltpu.make_async_copy(kv.at[kept], gathered_hbm.at[kept], keep_sem).wait()


def repair(
    attended_ref, over_ref, gathered_hbm, queries_hbm, lengths_hbm, out_hbm,
    kv, q_ref, o_ref, top, acc, lengths_ref, sem,
):
    copy = pltpu.make_async_copy(attended_ref, out_hbm, sem)
    copy.start()
    over = jnp.max(over_ref[...])
    copy.wait()

    @pl.when(over > 0.0)
    def _():
        seq = lax.axis_index("seq")
        chip = seq // 2
        load = pltpu.make_async_copy(gathered_hbm, kv, sem)
        load.start()
        load.wait()
        load = pltpu.make_async_copy(queries_hbm, q_ref, sem)
        load.start()
        load.wait()
        load = pltpu.make_async_copy(lengths_hbm, lengths_ref, sem)
        load.start()
        load.wait()
        shape = (ROWS, ROWS)
        row = seq * ROWS + lax.broadcasted_iota(jnp.int32, shape, 0)
        low = jnp.zeros(shape, jnp.int32)
        begin = jnp.int32(0)
        for number in range(NDOC):
            low = jnp.where(row >= begin, begin, low)
            begin = begin + lengths_ref[number]
        top[...] = jnp.full_like(top, -1e30)
        acc[...] = jnp.zeros_like(acc)

        @pl.loop(2 * jnp.maximum(chip - REACH, 0), seq + 1)
        def _(block):
            key = block * ROWS + lax.broadcasted_iota(jnp.int32, shape, 1)
            allowed = (key >= low) & (key <= row)
            keys = kv[block, :, 0].reshape(ROWS, DH)
            values = kv[block, :, 1].reshape(ROWS, DH)
            values = jnp.concatenate([values, jnp.ones_like(values)], axis=1)
            for h in range(HQ):
                queries = q_ref[:, h * DH:(h + 1) * DH]
                scores = lax.dot_general(queries, keys, NT, preferred_element_type=jnp.float32)
                old = top[h]
                peak = jnp.max(jnp.where(allowed, scores, -1e30), axis=1, keepdims=True)
                new = jnp.maximum(old, peak)
                top[h] = new
                fade = jnp.exp2((old - new) * SCALE)
                both = jnp.concatenate([new, new], axis=1)
                weights = jnp.where(allowed, jnp.exp2((scores - both) * SCALE), 0.0)
                acc[h] = acc[h] * jnp.concatenate([fade, fade], axis=1) + jnp.dot(
                    weights.astype(jnp.bfloat16), values, preferred_element_type=jnp.float32
                )

        for h in range(HQ):
            o_ref[:, h * DH:(h + 1) * DH] = (acc[h, :, :DH] / acc[h, :, DH:]).astype(jnp.bfloat16)
        again = pltpu.make_async_copy(o_ref, out_hbm, sem)
        again.start()
        again.wait()


def local(queries, keys, values, lengths):
    far_away = pl.BlockSpec(memory_space=pltpu.HBM)
    near = pl.BlockSpec(memory_space=pltpu.VMEM)
    attended, over, gathered = pl.pallas_call(
        kernel,
        out_shape=(
            pltpu.VMEM(queries.shape, jnp.bfloat16),
            pltpu.VMEM((8, DH), jnp.float32),
            jax.ShapeDtypeStruct((2 * CHIPS, 2, 2, HALF, DH), jnp.bfloat16),
        ),
        in_specs=[far_away] * 4,
        out_specs=(near, near, far_away),
        scratch_shapes=[
            pltpu.VMEM((ROWS, HQ * DH), jnp.bfloat16),
            pltpu.VMEM((2 * CHIPS, 2, 2, HALF, DH), jnp.bfloat16),
            pltpu.VMEM((CHIPS, 2, 2, HALF, DH), jnp.bfloat16),
            pltpu.VMEM((HQ + 1, ROWS, DH), jnp.bfloat16),
            pltpu.VMEM((HQ, ROWS, 2 * DH), jnp.float32),
            pltpu.SMEM((NDOC,), jnp.int32),
            pltpu.SemaphoreType.DMA,
            pltpu.SemaphoreType.DMA,
            pltpu.SemaphoreType.DMA,
            pltpu.SemaphoreType.DMA((2 * CHIPS,)),
            pltpu.SemaphoreType.DMA((2 * CHIPS,)),
            pltpu.SemaphoreType.DMA((len(OUT_WORDS), 3)),
            pltpu.SemaphoreType.DMA,
            pltpu.SemaphoreType.DMA,
        ],
        compiler_params=pltpu.CompilerParams(
            collective_id=0, has_side_effects=True, vmem_limit_bytes=1708 * 2**15
        ),
    )(queries, keys, values, lengths)
    return pl.pallas_call(
        repair,
        out_shape=jax.ShapeDtypeStruct(queries.shape, jnp.bfloat16),
        in_specs=[near] * 2 + [far_away] * 3,
        out_specs=far_away,
        scratch_shapes=[
            pltpu.VMEM((2 * CHIPS, 2, 2, HALF, DH), jnp.bfloat16),
            pltpu.VMEM((ROWS, HQ * DH), jnp.bfloat16),
            pltpu.VMEM((ROWS, HQ * DH), jnp.bfloat16),
            pltpu.VMEM((HQ, ROWS, DH), jnp.float32),
            pltpu.VMEM((HQ, ROWS, 2 * DH), jnp.float32),
            pltpu.SMEM((NDOC,), jnp.int32),
            pltpu.SemaphoreType.DMA,
        ],
        compiler_params=pltpu.CompilerParams(vmem_limit_bytes=1708 * 2**15),
    )(attended, over, gathered, queries, lengths)


def solution(mesh):
    placed = (P("seq", "head"), P("seq", "head"), P("seq", "head"), P())
    return jax.shard_map(
        local, mesh=mesh, in_specs=placed, out_specs=P("seq", "head"), check_vma=False
    )
```

```python
import math

import jax
import jax.numpy as jnp
from jax import lax
from jax.experimental import pallas as pl
from jax.experimental.pallas import tpu as pltpu
from jax.sharding import PartitionSpec as P

MESH = pl.DeviceIdType.MESH
HQ = 8
DH = 128
NDOC = 16
ROWS = 256
CHIPS = 16
HALF = ROWS // 2
FAR = -(2.0**20)
SCALE = math.log2(math.e) / math.sqrt(DH)
REACH = 9
BEHIND = 4
LIMIT = 2.0**100

FIRST = 3
WORK_WORDS = (
    (0, 0, 32771, 32772, 32774, 32777, 65856, 32780, 32768, 65616, 65683, 65748, 65846, 65880, 66384, 66044),
    (0, 0, 32770, 32773, 0, 32775, 0, 32770, 32769, 32785, 32773, 65778, 32791, 0, 66348, 66482),
    (0, 32768, 0, 0, 32773, 32776, 32769, 32779, 0, 65637, 32785, 0, 66221, 65913, 66091, 66413),
    (0, 32769, 0, 32771, 32775, 32768, 0, 32777, 65667, 65728, 66054, 66154, 66184, 66070, 66221, 32782),
    (0, 0, 0, 32770, 0, 32772, 65763, 32778, 65996, 65761, 65993, 66212, 65930, 66280, 65880, 66067),
    (0, 0, 32768, 0, 32772, 32769, 65605, 65574, 66018, 65679, 65810, 65705, 66002, 66124, 66043, 66362),
    (0, 0, 0, 32769, 65539, 32773, 32779, 65677, 65704, 65832, 65763, 65969, 65739, 65967, 66254, 66092),
    (0, 0, 32769, 0, 32770, 65638, 65832, 65768, 65901, 65870, 65922, 66056, 65779, 66101, 66290, 66197),
    (0, 0, 0, 32768, 32769, 32770, 65732, 65699, 65830, 65933, 65898, 65900, 66096, 66153, 66195, 66264),
    (0, 0, 0, 0, 0, 0, 0, 32768, 65863, 32779, 65967, 66030, 32783, 66190, 0, 32791),
)
IN_WORDS = (
    (32771, 118214, 163843, 252164, 196998, 163849, 328000, 163852, 197280, 327760, 327827, 327892, 327990, 328024, 504656, 328188),
    (0, 32783, 196866, 163845, 0, 163847, 32782, 163842, 163841, 197265, 163845, 327922, 163863, 0, 163865, 328626),
    (0, 196736, 0, 0, 163845, 197032, 163841, 163851, 32788, 327781, 163857, 0, 500397, 328057, 505387, 506733),
    (0, 197313, 0, 196963, 163847, 163840, 0, 163849, 503939, 327872, 501254, 496234, 504148, 328214, 502549, 0),
    (0, 32780, 0, 163842, 0, 163844, 327907, 163850, 506958, 507105, 500302, 496949, 163858, 504552, 506363, 518675),
    (0, 0, 163840, 0, 163844, 163841, 502853, 504870, 505000, 163844, 493795, 500145, 498030, 505330, 0, 360857),
    (0, 0, 0, 163841, 327683, 163845, 0, 327940, 327883, 506152, 328012, 503184, 327923, 501301, 328278, 328369),
    (0, 0, 163841, 0, 163842, 327782, 327976, 163847, 0, 504234, 328171, 163854, 163856, 328147, 328311, 328468),
    (0, 0, 0, 163840, 163841, 163842, 327876, 491683, 327913, 0, 163853, 163855, 328177, 163860, 163860, 328438),
    (0, 0, 0, 0, 0, 0, 0, 0, 163850, 163851, 0, 0, 0, 0, 0, 0),
)
OUT_WORDS = (
    (268550144, 461915747, 268552292, 462949478, 463753321, 268555370, 464525420, 268557966, 268443760, 268559987, 268446324, 268561526, 134217848, 134217850, 134217852, 0),
    (134217953, 268436578, 454412901, 268553863, 134217736, 134217995, 268524301, 268508718, 134217841, 268444818, 134217780, 134217847, 134217881, 0, 134217853, 0),
    (268436064, 268535523, 268503588, 134217926, 268554344, 447338123, 268556845, 134217966, 268444305, 0, 268445845, 0, 134217849, 134217883, 0, 0),
    (134217825, 449715430, 134217827, 462433383, 268570860, 268441225, 268555296, 134217998, 268446304, 134217840, 268437619, 134217844, 268440182, 268457080, 268507184, 0),
    (134217731, 134217967, 446812258, 268552836, 0, 134217831, 448388202, 134217868, 268460129, 268452978, 134217845, 268439154, 268456567, 134217851, 268458106, 268459631),
    (0, 268438624, 268538082, 268554340, 268553349, 134217965, 268452449, 472766498, 134217760, 268454499, 268454001, 268510247, 134217773, 134217771, 268555897, 464789101),
    (0, 465045633, 0, 455988835, 268553829, 463802400, 0, 0, 268507185, 134217766, 268456560, 268457075, 268458101, 134217846, 268460661, 134217778),
    (0, 450484321, 0, 134217826, 134217830, 134217832, 268453479, 268571177, 0, 268445807, 134217838, 268440723, 0, 268460151, 268459128, 268507699),
    (0, 134217731, 134217824, 134217899, 0, 268452452, 268452965, 268571686, 134217748, 268508711, 0, 268458609, 134217844, 268512815, 0, 134217952),
)
EDGES = ((-2, 0), (-2, 1), (-1, 0), (-1, 1), (0, 1), (1, 0), (1, 1), (2, 0))

NT = (((1,), (1,)), ((), ()))


def pick(table, index, default):
    value = jnp.int32(default)
    for number, entry in enumerate(table):
        value = jnp.where(index == number, entry, value)
    return value


def kernel(
    queries_hbm, keys_hbm, values_hbm, lengths_hbm, out_ref, over_ref, gathered_hbm,
    q_ref, kv, far, mine, acc, lengths_ref,
    q_sem, own_sem, lengths_sem, recv_sem, sib_recv, send_sem, sib_send, keep_sem,
):
    seq, head = lax.axis_index("seq"), lax.axis_index("head")
    core = seq % 2
    chip = seq // 2
    z = chip % 8
    high = chip // 8
    own = 2 * chip + core

    def device(flip, move, core):
        side = high + flip - 2 * high * flip
        return (side * 16 + ((z + move + 8) % 8) * 2 + core, head)

    sibling = device(0, 0, 1 - core)
    barrier = pltpu.get_barrier_semaphore()
    partners = sorted({(m, f) for m, f in EDGES} | {(-m, f) for m, f in EDGES})
    for move, flip in partners:
        pl.semaphore_signal(barrier, inc=1, device_id=device(flip, move, core), device_id_type=MESH)
    pl.semaphore_signal(barrier, inc=1, device_id=sibling, device_id_type=MESH)

    load_lengths = pltpu.make_async_copy(lengths_hbm, lengths_ref, lengths_sem)
    load_lengths.start()
    for half in range(2):
        part = pl.ds(half * HALF, HALF)
        pltpu.make_async_copy(keys_hbm.at[part], kv.at[own, half, 0], own_sem).start()
        pltpu.make_async_copy(values_hbm.at[part], kv.at[own, half, 1], own_sem).start()
    load_q = pltpu.make_async_copy(queries_hbm, q_ref, q_sem)
    load_q.start()

    ins = [pick(row, chip, 0) for row in IN_WORDS]
    outs = [pick(row, chip, 0) for row in OUT_WORDS]
    works = [pick(row, chip, 0) for row in WORK_WORDS]

    load_lengths.wait()
    lane = lax.broadcasted_iota(jnp.int32, (1, DH), 1)
    first = jnp.zeros((1, DH), jnp.int32)
    last = jnp.zeros((1, DH), jnp.int32)
    begin = jnp.int32(0)
    for number in range(NDOC):
        end = begin + lengths_ref[number]
        first = jnp.where(lane == number, begin, first)
        last = jnp.where(lane == number, end, last)
        begin = end
    row_pos = own * ROWS + lax.broadcasted_iota(jnp.int32, (ROWS, DH), 0)
    mark = ((row_pos >= first) & (row_pos < last)).astype(jnp.float32)
    mine[0] = mark.astype(jnp.bfloat16)
    low = jnp.where(lane < NDOC, first, 0)
    top_pos = jnp.where(lane < NDOC, last, 2 * ROWS * CHIPS)

    pltpu.make_async_copy(kv.at[own], kv.at[own], own_sem).wait()
    pl.semaphore_wait(barrier, len(partners) + 1)

    def sib_copy(item, side, sem):
        part = kv.at[2 * (item // 2) + side, item % 2]
        return pltpu.make_async_remote_copy(
            src_ref=part, dst_ref=part, send_sem=sem, recv_sem=sib_recv.at[item],
            device_id=sibling, device_id_type=MESH,
        )

    def edge_copy(item, target, sem):
        part = kv.at[2 * (item // 2) + core, item % 2]
        return pltpu.make_async_remote_copy(
            src_ref=part, dst_ref=part, send_sem=sem, recv_sem=recv_sem.at[item],
            device_id=target, device_id_type=MESH,
        )

    def receive(step, word):
        arrive, needed = (word // 2**15) % 4, word // 2**17
        for place in range(3):
            item = (word // 32**place) % 32

            @pl.when(place < arrive)
            def _():
                edge_copy(item, sibling, send_sem.at[0, 0]).wait_recv()

            @pl.when(place < needed)
            def _():
                sib_copy(item, core, sib_send).start()

    def forward(step, word):
        for place in range(3):
            entry = (word // 512**place) % 512
            edge = entry // 32

            @pl.when(place < word // 512**3)
            def _():
                target = device(edge // 5, edge % 5 - 2, core)
                edge_copy(entry % 32, target, send_sem.at[step, place]).start()

    def keep(item, sem):
        at = (pl.ds(2 * (item // 2), 2), item % 2)
        return pltpu.make_async_copy(kv.at[at], gathered_hbm.at[at], sem)

    def settle(step, word):
        for place in range(3):
            @pl.when(place < word // 512**3)
            def _():
                edge_copy(own, sibling, send_sem.at[step, place]).wait_send()

    for step in range(FIRST):
        forward(step, outs[step])
    for half in range(2):
        sib_copy(2 * chip + half, core, sib_send).start()

    def load_keys(item):
        both = kv[pl.ds(2 * (item // 2), 2), item % 2, 0].reshape(ROWS, DH)
        away = far[item // 2, item % 2].reshape(ROWS, DH)
        return jnp.concatenate([both, away], axis=1)

    def load_values(item):
        both = kv[pl.ds(2 * (item // 2), 2), item % 2, 1].reshape(ROWS, DH)
        return jnp.concatenate([both, jnp.ones_like(both)], axis=1)

    def load_queries(h, which):
        return jnp.concatenate([q_ref[:, h * DH:(h + 1) * DH], mine[which]], axis=1)

    def product(h, which, items):
        keys = jnp.concatenate([load_keys(item) for item in items], axis=0)
        return lax.dot_general(load_queries(h, which), keys, NT, preferred_element_type=jnp.float32)

    def mix(weights, items):
        values = jnp.concatenate([load_values(item) for item in items], axis=0)
        return jnp.dot(weights, values, preferred_element_type=jnp.float32)

    def absorb(items):
        weights = None
        for h in range(HQ + 1):
            ready = weights
            if h < HQ:
                weights = jnp.exp2(product(h, h + 1, items) * SCALE).astype(jnp.bfloat16)
            if h >= 1:
                acc[h - 1] += mix(ready, items)

    @pl.loop(jnp.maximum(chip - REACH, 0), chip + 1)
    def _(block):
        for side in range(2):
            for half in range(2):
                at = block * 2 * ROWS + side * ROWS + half * HALF
                pos = at + lax.broadcasted_iota(jnp.int32, (HALF, DH), 0)
                inside = (pos >= low) & (pos < top_pos)
                away = jnp.where(inside, (lane == NDOC).astype(jnp.float32), FAR)
                far[block, half, side] = away.astype(jnp.bfloat16)

    load_q.wait()
    for half in range(2):
        sib_copy(2 * chip + half, 1 - core, sib_send).wait_recv()
    shape = (ROWS, 2 * ROWS)
    column = lax.broadcasted_iota(jnp.int32, shape, 1)
    column = (column // ROWS) * HALF + ((column // HALF) % 2) * ROWS + column % HALF
    causal = column <= core * ROWS + lax.broadcasted_iota(jnp.int32, shape, 0)
    items = [2 * chip, 2 * chip + 1]
    for half in range(2):
        keep(items[half], keep_sem).start()
    for h in range(HQ):
        scores = jnp.where(causal, product(h, 0, items), -1e30)
        shift = jnp.max(scores, axis=1, keepdims=True).astype(jnp.bfloat16).astype(jnp.float32)
        mine[h + 1] = jnp.where(lane == NDOC, -shift, mark).astype(jnp.bfloat16)
        weights = jnp.exp2((scores - shift) * SCALE).astype(jnp.bfloat16)
        acc[h] = mix(weights, items)

    @pl.loop(FIRST, FIRST + 1 + len(WORK_WORDS))
    def _(step):
        arrived = pick(ins, step - FIRST, 0)
        receive(step, arrived)
        forward(step, pick(outs, step, 0))

        settle(step - BEHIND, pick(outs, step - BEHIND, 0))

        word = pick(works, step - 1 - FIRST, 0)
        needed = word // 2**15
        items = [(word // 32**place) % 32 for place in range(3)]
        for place in range(3):
            @pl.when(place < needed)
            def _():
                sib_copy(items[place], 1 - core, sib_send).wait_recv()
                keep(items[place], keep_sem).start()

        for count in range(1, 4):
            @pl.when(needed == count)
            def _():
                absorb(items[:count])

    over = jnp.zeros((ROWS, DH), jnp.float32)
    for h in range(HQ):
        total = acc[h, :, DH:]
        over = jnp.where(total < LIMIT, over, 1.0)
        out_ref[:, h * DH:(h + 1) * DH] = (acc[h, :, :DH] / total).astype(jnp.bfloat16)
    over_ref[...] = jnp.max(over.reshape(ROWS // 8, 8, DH), axis=0)

    for step in range(FIRST + 1 + len(WORK_WORDS) - BEHIND, len(OUT_WORDS)):
        settle(step, outs[step])

    for count in range(1, REACH + 2):
        @pl.when(jnp.minimum(chip, REACH) + 1 == count)
        def _():
            blocks = kv.at[pl.ds(0, count)]
            pltpu.make_async_remote_copy(
                src_ref=blocks, dst_ref=blocks, send_sem=sib_send, recv_sem=sib_recv.at[0],
                device_id=sibling, device_id_type=MESH,
            ).wait_send()
            kept = pl.ds(0, 2 * count)
            pltpu.make_async_copy(kv.at[kept], gathered_hbm.at[kept], keep_sem).wait()


def repair(
    attended_ref, over_ref, gathered_hbm, queries_hbm, lengths_hbm, out_hbm,
    kv, q_ref, o_ref, top, acc, lengths_ref, sem,
):
    copy = pltpu.make_async_copy(attended_ref, out_hbm, sem)
    copy.start()
    over = jnp.max(over_ref[...])
    copy.wait()

    @pl.when(over > 0.0)
    def _():
        seq = lax.axis_index("seq")
        chip = seq // 2
        load = pltpu.make_async_copy(gathered_hbm, kv, sem)
        load.start()
        load.wait()
        load = pltpu.make_async_copy(queries_hbm, q_ref, sem)
        load.start()
        load.wait()
        load = pltpu.make_async_copy(lengths_hbm, lengths_ref, sem)
        load.start()
        load.wait()
        shape = (ROWS, ROWS)
        row = seq * ROWS + lax.broadcasted_iota(jnp.int32, shape, 0)
        low = jnp.zeros(shape, jnp.int32)
        begin = jnp.int32(0)
        for number in range(NDOC):
            low = jnp.where(row >= begin, begin, low)
            begin = begin + lengths_ref[number]
        top[...] = jnp.full_like(top, -1e30)
        acc[...] = jnp.zeros_like(acc)

        @pl.loop(2 * jnp.maximum(chip - REACH, 0), seq + 1)
        def _(block):
            key = block * ROWS + lax.broadcasted_iota(jnp.int32, shape, 1)
            allowed = (key >= low) & (key <= row)
            keys = kv[block, :, 0].reshape(ROWS, DH)
            values = kv[block, :, 1].reshape(ROWS, DH)
            values = jnp.concatenate([values, jnp.ones_like(values)], axis=1)
            for h in range(HQ):
                queries = q_ref[:, h * DH:(h + 1) * DH]
                scores = lax.dot_general(queries, keys, NT, preferred_element_type=jnp.float32)
                old = top[h]
                peak = jnp.max(jnp.where(allowed, scores, -1e30), axis=1, keepdims=True)
                new = jnp.maximum(old, peak)
                top[h] = new
                fade = jnp.exp2((old - new) * SCALE)
                both = jnp.concatenate([new, new], axis=1)
                weights = jnp.where(allowed, jnp.exp2((scores - both) * SCALE), 0.0)
                acc[h] = acc[h] * jnp.concatenate([fade, fade], axis=1) + jnp.dot(
                    weights.astype(jnp.bfloat16), values, preferred_element_type=jnp.float32
                )

        for h in range(HQ):
            o_ref[:, h * DH:(h + 1) * DH] = (acc[h, :, :DH] / acc[h, :, DH:]).astype(jnp.bfloat16)
        again = pltpu.make_async_copy(o_ref, out_hbm, sem)
        again.start()
        again.wait()


def local(queries, keys, values, lengths):
    far_away = pl.BlockSpec(memory_space=pltpu.HBM)
    near = pl.BlockSpec(memory_space=pltpu.VMEM)
    attended, over, gathered = pl.pallas_call(
        kernel,
        out_shape=(
            pltpu.VMEM(queries.shape, jnp.bfloat16),
            pltpu.VMEM((8, DH), jnp.float32),
            jax.ShapeDtypeStruct((2 * CHIPS, 2, 2, HALF, DH), jnp.bfloat16),
        ),
        in_specs=[far_away] * 4,
        out_specs=(near, near, far_away),
        scratch_shapes=[
            pltpu.VMEM((ROWS, HQ * DH), jnp.bfloat16),
            pltpu.VMEM((2 * CHIPS, 2, 2, HALF, DH), jnp.bfloat16),
            pltpu.VMEM((CHIPS, 2, 2, HALF, DH), jnp.bfloat16),
            pltpu.VMEM((HQ + 1, ROWS, DH), jnp.bfloat16),
            pltpu.VMEM((HQ, ROWS, 2 * DH), jnp.float32),
            pltpu.SMEM((NDOC,), jnp.int32),
            pltpu.SemaphoreType.DMA,
            pltpu.SemaphoreType.DMA,
            pltpu.SemaphoreType.DMA,
            pltpu.SemaphoreType.DMA((2 * CHIPS,)),
            pltpu.SemaphoreType.DMA((2 * CHIPS,)),
            pltpu.SemaphoreType.DMA((len(OUT_WORDS), 3)),
            pltpu.SemaphoreType.DMA,
            pltpu.SemaphoreType.DMA,
        ],
        compiler_params=pltpu.CompilerParams(
            collective_id=0, has_side_effects=True, vmem_limit_bytes=1708 * 2**15
        ),
    )(queries, keys, values, lengths)
    return pl.pallas_call(
        repair,
        out_shape=jax.ShapeDtypeStruct(queries.shape, jnp.bfloat16),
        in_specs=[near] * 2 + [far_away] * 3,
        out_specs=far_away,
        scratch_shapes=[
            pltpu.VMEM((2 * CHIPS, 2, 2, HALF, DH), jnp.bfloat16),
            pltpu.VMEM((ROWS, HQ * DH), jnp.bfloat16),
            pltpu.VMEM((ROWS, HQ * DH), jnp.bfloat16),
            pltpu.VMEM((HQ, ROWS, DH), jnp.float32),
            pltpu.VMEM((HQ, ROWS, 2 * DH), jnp.float32),
            pltpu.SMEM((NDOC,), jnp.int32),
            pltpu.SemaphoreType.DMA,
        ],
        compiler_params=pltpu.CompilerParams(vmem_limit_bytes=1708 * 2**15),
    )(attended, over, gathered, queries, lengths)


def solution(mesh):
    placed = (P("seq", "head"), P("seq", "head"), P("seq", "head"), P())
    return jax.shard_map(
        local, mesh=mesh, in_specs=placed, out_specs=P("seq", "head"), check_vma=False
    )
```
